32 devices in a mesh: ctx: 8 (over z, x), ch: 4 (over y, core).
Axes of the slice: x: 2, y: 2, z: 4, core: 2. Of those that a mesh axis runs over, the one named last changes fastest.
Arguments:
- tokens: bfloat16 [4096, 8192], P('ctx'), may hold values from -6 to 6
- in_weight: bfloat16 [8192, 3, 4096], P('ctx', None, 'ch'), may hold values from -0.0625 to 0.0625
- short_taps: float32 [3, 3, 4096], P(None, None, 'ch'), may hold values from -3 to 3
- decay_rates: float32 [16, 4096], P(None, 'ch'), may hold values from 0 to 0.034, as said below
- residues: float32 [16, 4096], P(None, 'ch'), may hold values from -1.5 to 1.5
Outputs:
- mixed: bfloat16 [4096, 4096], P(('ctx', 'ch'))
The draws below stay inside these ranges and needn't reach their ends.
Inputs may be any that keep to these rules, and one draw needn't show every extreme that they name: `decay_rates`: positive decay rates.
All inputs are finite; a program needn't handle non-finite values.
Results may differ from the reference program's by a relative error of at most 0.0063.
Values may be sent and summed in bfloat16 or wider, within the bound.
No kernel may reach another device: no remote copies, remote signals or barrier semaphores. Data moves between devices by JAX's collectives and lax.ppermute only.
A program may use at most 128 MiB of HBM per device.

```python
import jax
import jax.numpy as jnp
from jax import lax

D = 8192
DCONV = 4096
M = 16
TOKENS = 4096


def draw_decay_rates(key, part):
    pick_key, slow_key, mid_key, fast_key = jax.random.split(key, 4)
    dims = (M, DCONV)
    chooser = jax.random.uniform(pick_key, dims)
    slow = jnp.exp(jax.random.uniform(slow_key, dims, minval=jnp.log(0.05 / TOKENS), maxval=jnp.log(2.0 / TOKENS)))
    middle = jnp.exp(jax.random.uniform(mid_key, dims, minval=jnp.log(2.0 / TOKENS), maxval=jnp.log(1.0 / 50.0)))
    fast = jnp.exp(jax.random.uniform(fast_key, dims, minval=jnp.log(1.0 / 50.0), maxval=jnp.log(1.0 / 30.0)))
    slow_share = 0.5
    mid_share = 0.7
    return jnp.where(chooser < slow_share, slow, jnp.where(chooser < mid_share, middle, fast)).astype(jnp.float32)


def levels(own_key, extent, cuts, smallest, high):
    factor_of = 1.0
    for position, blocks in cuts:
        draws = jax.random.uniform(jax.random.fold_in(jax.random.fold_in(own_key, 6), position), (blocks,), jnp.float32, smallest / len(cuts), high / len(cuts))
        factor_of = factor_of * jnp.repeat(jnp.exp(draws), extent[position] // blocks).reshape((-1,) + (1,) * (len(extent) - 1 - position))
    return factor_of


def gaussian(stream_key, shape, spread, bound, cuts=(), held_as=jnp.bfloat16):
    drawn = jax.random.normal(stream_key, shape, jnp.float32) * spread
    if len(cuts) > 0:
        drawn = levels(stream_key, shape, cuts, -0.22, 0.18) * drawn
    return jnp.clip(drawn, min=-bound, max=bound).astype(held_as)


def setup_inputs(seed: int = 0) -> dict:
    splits = jax.random.split(jax.random.key(seed), 6)
    tokens = gaussian(splits[0], (TOKENS, D), 1.0, 6.0, ((0, 8),))
    in_weight = gaussian(splits[1], (D, 3, DCONV), D ** -0.5, 0.0625, ((0, 8), (2, 4)))
    short_taps = gaussian(splits[2], (3, 3, DCONV), 0.5, 3.0, ((2, 4),), jnp.float32)
    decay_rates = draw_decay_rates(jax.random.fold_in(splits[5], 71), 0)
    residues = gaussian(splits[4], (M, DCONV), 0.25, 1.5, ((1, 4),), jnp.float32)
    return dict(tokens=tokens, in_weight=in_weight, short_taps=short_taps, decay_rates=decay_rates, residues=residues)


def reference(tokens, in_weight, short_taps, decay_rates, residues):
    flat_weight = in_weight.reshape(D, 3 * DCONV)
    projected = jnp.dot(tokens, flat_weight, preferred_element_type=jnp.float32).astype(jnp.bfloat16)
    projected = projected.reshape(TOKENS, 3, DCONV).astype(jnp.float32)
    padded = jnp.concatenate([jnp.zeros((2, 3, DCONV), jnp.float32), projected], axis=0)
    featurized = short_taps[0] * padded[2:] + short_taps[1] * padded[1:-1] + short_taps[2] * padded[:-2]
    query_part = featurized[:, 0]
    product = featurized[:, 1] * featurized[:, 2]
    decay = jnp.exp(-decay_rates)
    scaled = residues * jnp.sqrt(2.0 * decay_rates)

    def advance(state, entry):
        state = decay * state + entry[None, :]
        return (state, lax.optimization_barrier(jnp.sum(scaled * state, axis=0)))
    last_state, conv_out = lax.scan(advance, jnp.zeros((M, DCONV), jnp.float32), product)
    return (query_part * conv_out).astype(jnp.bfloat16)
```

```python
import functools

import jax
import jax.numpy as jnp
from jax import lax
from jax.experimental import pallas as pl
from jax.experimental.pallas import tpu as pltpu
from jax.sharding import Mesh
from jax.sharding import PartitionSpec as P


def conv_kernel(order, proj, taps, decay, scaled, state_in, halo_in, out, state, halo, ext, prod, modes):
    rows, width = out.shape[1], out.shape[2]
    mode_count = decay.shape[0]

    @pl.when(pl.program_id(0) == 0)
    def _():
        state[...] = state_in[...]
        halo[...] = halo_in[...]

    ext[0:8, :] = halo[...]
    ext[8 : 8 + rows, :] = proj[0].astype(jnp.float32)
    halo[...] = ext[rows : rows + 8, :]

    def branch(i):
        cols = slice(i * width, (i + 1) * width)
        return (
            taps[0:1, cols] * ext[8 : 8 + rows, cols]
            + taps[1:2, cols] * ext[7 : 7 + rows, cols]
            + taps[2:3, cols] * ext[6 : 6 + rows, cols]
        )

    prod[...] = branch(1) * branch(2)
    halves = [slice(s, s + 8) for s in range(0, mode_count, 8)]
    decays = [decay[h, :] for h in halves]
    scales = [scaled[h, :] for h in halves]

    def step(t, states):
        entry = jnp.broadcast_to(prod[pl.ds(t, 1), :], (8, width))
        states = tuple(d * s + entry for d, s in zip(decays, states))
        total = scales[0] * states[0]
        for c, s in zip(scales[1:], states[1:]):
            total = total + c * s
        modes[pl.ds(pl.multiple_of(t * 8, 8), 8), :] = total
        return states

    states = lax.fori_loop(0, rows, step, tuple(state[h, :] for h in halves), unroll=8)
    for h, s in zip(halves, states):
        state[h, :] = s
    conv = modes[pl.ds(0, rows, stride=8), :]
    for s in range(1, 8):
        conv = conv + modes[pl.ds(s, rows, stride=8), :]
    out[0] = (branch(0) * conv).astype(out.dtype)


def run_conv(order, proj, taps, decay, scaled, state, halo):
    blocks, rows, width3 = proj.shape
    width = width3 // 3
    mode_count = decay.shape[0]
    whole = lambda shape: pl.BlockSpec(shape, lambda i, order: (0,) * len(shape))
    return pl.pallas_call(
        conv_kernel,
        out_shape=(
            jax.ShapeDtypeStruct((blocks, rows, width), jnp.bfloat16),
            jax.ShapeDtypeStruct((mode_count, width), jnp.float32),
            jax.ShapeDtypeStruct((8, width3), jnp.float32),
        ),
        grid_spec=pltpu.PrefetchScalarGridSpec(
            num_scalar_prefetch=1,
            grid=(blocks,),
            in_specs=[
                pl.BlockSpec((1, rows, width3), lambda i, order: (order[i], 0, 0)),
                whole((3, width3)),
                whole((mode_count, width)),
                whole((mode_count, width)),
                whole((mode_count, width)),
                whole((8, width3)),
            ],
            out_specs=[
                pl.BlockSpec((1, rows, width), lambda i, order: (i, 0, 0)),
                whole((mode_count, width)),
                whole((8, width3)),
            ],
            scratch_shapes=[
                pltpu.VMEM((rows + 8, width3), jnp.float32),
                pltpu.VMEM((rows, width), jnp.float32),
                pltpu.VMEM((rows * 8, width), jnp.float32),
            ],
        ),
        compiler_params=pltpu.CompilerParams(vmem_limit_bytes=24 * 1024 * 1024),
        cost_estimate=pl.CostEstimate(
            flops=8 * blocks * rows * mode_count * width,
            bytes_accessed=blocks * rows * width * 8,
            transcendentals=0,
        ),
    )(order, proj, taps, decay, scaled, state, halo)


def gather_rel(value, axis):
    count = lax.axis_size(axis)
    pieces = [value]
    for k in range(1, count):
        pieces.append(lax.ppermute(value, axis, [(s, (s + k) % count) for s in range(count)]))
    return jnp.concatenate(pieces, axis=0) if count > 1 else value


def shards(tokens, in_weight, short_taps, decay_rates, residues):
    Z, X, Y, C = (lax.axis_size(a) for a in ("z", "x", "y", "c"))
    z, x, y, c = (lax.axis_index(a) for a in ("z", "x", "y", "c"))
    tok_rows, depth = tokens.shape
    w_rows, _, chans = in_weight.shape
    own = chans // X
    half = own // 2
    groups = max(1, half // 128)
    width = half // groups
    plane_depth = X * w_rows

    lower = z < Z // 2
    far_off = jnp.where(lower, 0, half)
    near_off = half - far_off

    weight = jnp.transpose(in_weight, (1, 0, 2))

    def part(target, g):
        cuts = [
            lax.dynamic_slice(weight, (i, 0, target * own + off + g * width), (1, w_rows, width))[0]
            for off in (far_off, near_off)
            for i in range(3)
        ]
        return jnp.concatenate(cuts, axis=1)

    weights = []
    for g in range(groups):
        held = jnp.zeros((X, w_rows, 6 * width), in_weight.dtype)
        held = lax.dynamic_update_slice(held, part(x, g)[None], (x, 0, 0))
        for k in range(1, X):
            got = lax.ppermute(
                part((x + k) % X, g), "x", [(s, (s + k) % X) for s in range(X)]
            )
            held = lax.dynamic_update_slice(held, got[None], ((x + X - k) % X, 0, 0))
        weights.append(held.reshape(plane_depth, 6 * width))

    share = tok_rows // (Y * C)
    mine = lax.dynamic_slice(tokens, ((y * C + c) * share, 0), (share, depth))
    mine = mine.reshape(share, Z, plane_depth).transpose(1, 0, 2)
    split = lax.all_to_all(mine, "z", split_axis=0, concat_axis=0, tiled=True)

    bx, by, bc = jnp.meshgrid(jnp.arange(X), jnp.arange(Y), jnp.arange(C), indexing="ij")
    order = (((c - bc) % C) * Y + (y - by) % Y) * X + (x - bx) % X
    order = order.reshape(-1).astype(jnp.int32)

    def near_cut(value, g):
        return lax.dynamic_slice_in_dim(value, x * own + near_off + g * width, width, axis=value.ndim - 1)

    scaled_all = residues * jnp.sqrt(2.0 * decay_rates)
    decay_all = jnp.exp(-decay_rates)
    taps = [near_cut(short_taps, g).reshape(3, 3 * width) for g in range(groups)]
    decay = [near_cut(decay_all, g) for g in range(groups)]
    scaled = [near_cut(scaled_all, g) for g in range(groups)]
    state = [jnp.zeros_like(d) for d in decay]
    halo = [jnp.zeros((8, 3 * width), jnp.float32) for _ in range(groups)]

    outs = []
    for zt in range(Z):
        block = gather_rel(gather_rel(gather_rel(split[zt], "x"), "y"), "c")
        per_group = []
        for g in range(groups):
            partial = jnp.dot(block, weights[g], preferred_element_type=jnp.float32)
            far, near = partial[:, : 3 * width], partial[:, 3 * width :]
            got = None
            for hop in range(1, Z):
                send = far if hop <= Z // 2 else near
                if got is not None:
                    send = send + got.astype(jnp.float32)
                got = lax.ppermute(
                    send.astype(jnp.bfloat16), "z", [(hop - 1, hop), (Z - hop, Z - 1 - hop)]
                )
            total = (near + got.astype(jnp.float32)).astype(jnp.bfloat16)
            total = total.reshape(X * Y * C, share, 3 * width)
            out, state[g], halo[g] = run_conv(order, total, taps[g], decay[g], scaled[g], state[g], halo[g])
            per_group.append(out)
        outs.append(jnp.concatenate(per_group, axis=2))

    result = jnp.stack(outs).reshape(Z * X * Y * C, share, half)
    result = lax.all_to_all(result, ("z", "x", "y", "c"), split_axis=0, concat_axis=0, tiled=True)
    result = result.reshape(Z, X, Y, C, share, half)
    result = jnp.stack([result[Z - 1], result[0]])
    return result.transpose(4, 2, 3, 1, 0, 5).reshape(share, -1)


def solution(mesh):
    ctx, ch = mesh.shape["ctx"], mesh.shape["ch"]
    xs = 1
    while 4 * xs * xs <= ctx:
        xs *= 2
    cs = 2 if ch % 2 == 0 else 1
    fine = Mesh(mesh.devices.reshape(ctx // xs, xs, ch // cs, cs), ("z", "x", "y", "c"))
    return jax.shard_map(
        shards,
        mesh=fine,
        in_specs=(
            P(("z", "x"), None),
            P(("z", "x"), None, ("y", "c")),
            P(None, None, ("y", "c")),
            P(None, ("y", "c")),
            P(None, ("y", "c")),
        ),
        out_specs=P(("z", "x", "y", "c"), None),
        check_vma=False,
    )
```

```python
import functools
import math

import jax
import jax.numpy as jnp
from jax import lax
from jax.experimental import pallas as pl
from jax.experimental.pallas import tpu as pltpu
from jax.sharding import Mesh
from jax.sharding import PartitionSpec as P


def conv_kernel(order, pick, *refs):
    parts = refs[:-11]
    taps, decay, scaled, state_in, halo_in, out, state, halo, ext, prod, modes = refs[-11:]
    rows, width = out.shape[1], out.shape[2]
    mode_count = decay.shape[0]
    tiles, _, lane = modes.shape
    i = pl.program_id(0)

    @pl.when(i == 0)
    def _():
        state[...] = state_in[...]
        halo[...] = halo_in[...]

    ext[0:8, :] = halo[...]
    for p, value in enumerate(parts):

        @pl.when(pick[i] == p)
        def _(value=value):
            ext[8 : 8 + rows, :] = value[0]

    halo[...] = ext[rows : rows + 8, :]

    def branch(i):
        cols = slice(i * width, (i + 1) * width)
        return (
            taps[0:1, cols] * ext[8 : 8 + rows, cols]
            + taps[1:2, cols] * ext[7 : 7 + rows, cols]
            + taps[2:3, cols] * ext[6 : 6 + rows, cols]
        )

    prod[...] = branch(1) * branch(2)
    halves = [slice(s, s + 8) for s in range(0, mode_count, 8)]
    decays = [decay[h, :] for h in halves]
    scales = [scaled[h, :] for h in halves]

    def step(t, states):
        entry = jnp.broadcast_to(prod[pl.ds(t, 1), :], (8, width))
        states = tuple(d * s + entry for d, s in zip(decays, states))
        total = scales[0] * states[0]
        for c, s in zip(scales[1:], states[1:]):
            total = total + c * s
        for i in range(tiles):
            modes[i, pl.ds(pl.multiple_of(t * 8, 8), 8), :] = total[:, i * lane : (i + 1) * lane]
        return states

    states = lax.fori_loop(0, rows, step, tuple(state[h, :] for h in halves), unroll=8)
    for h, s in zip(halves, states):
        state[h, :] = s
    gate = branch(0)
    for i in range(tiles):
        cols = slice(i * lane, (i + 1) * lane)
        conv = modes[i, pl.ds(0, rows, stride=8), :]
        for s in range(1, 8):
            conv = conv + modes[i, pl.ds(s, rows, stride=8), :]
        out[0, :, cols] = (gate[:, cols] * conv).astype(out.dtype)


def run_conv(order, pick, parts, rows, taps, decay, scaled, state, halo):
    blocks = order.shape[0]
    width3 = taps.shape[1]
    width = width3 // 3
    mode_count = decay.shape[0]
    lane = min(128, width)

    def whole(shape):
        return pl.BlockSpec(shape, lambda i, order, pick: (0,) * len(shape))

    return pl.pallas_call(
        conv_kernel,
        out_shape=(
            jax.ShapeDtypeStruct((blocks, rows, width), jnp.bfloat16),
            jax.ShapeDtypeStruct((mode_count, width), jnp.float32),
            jax.ShapeDtypeStruct((8, width3), jnp.float32),
        ),
        grid_spec=pltpu.PrefetchScalarGridSpec(
            num_scalar_prefetch=2,
            grid=(blocks,),
            in_specs=[pl.BlockSpec((1, rows, width3), lambda i, order, pick: (order[i], 0, 0))] * len(parts)
            + [
                whole((3, width3)),
                whole((mode_count, width)),
                whole((mode_count, width)),
                whole((mode_count, width)),
                whole((8, width3)),
            ],
            out_specs=[
                pl.BlockSpec((1, rows, width), lambda i, order, pick: (i, 0, 0)),
                whole((mode_count, width)),
                whole((8, width3)),
            ],
            scratch_shapes=[
                pltpu.VMEM((rows + 8, width3), jnp.float32),
                pltpu.VMEM((rows, width), jnp.float32),
                pltpu.VMEM((width // lane, rows * 8, lane), jnp.float32),
            ],
        ),
        compiler_params=pltpu.CompilerParams(vmem_limit_bytes=24 * 1024 * 1024),
        cost_estimate=pl.CostEstimate(
            flops=8 * blocks * rows * mode_count * width,
            bytes_accessed=blocks * rows * width * 20,
            transcendentals=0,
        ),
        name="conv",
    )(order, pick, *(p.reshape(-1, rows, width3) for p in parts), taps, decay, scaled, state, halo)


def copy_kernel(cuts, first, source, target, sems):
    copies = [
        pltpu.make_async_copy(take(source, first[0]), put(target), sems.at[i]) for i, (take, put) in enumerate(cuts)
    ]
    for copy in copies:
        copy.start()
    for copy in copies:
        copy.wait()


def copy_cuts(name, cuts, shape, first, source):
    anywhere = pl.BlockSpec(memory_space=pl.ANY)
    return pl.pallas_call(
        functools.partial(copy_kernel, cuts),
        out_shape=jax.ShapeDtypeStruct(shape, source.dtype),
        in_specs=[pl.BlockSpec(memory_space=pltpu.SMEM), anywhere],
        out_specs=anywhere,
        scratch_shapes=[pltpu.SemaphoreType.DMA((len(cuts),))],
        compiler_params=pltpu.CompilerParams(vmem_limit_bytes=48 * 1024 * 1024),
        cost_estimate=pl.CostEstimate(flops=0, bytes_accessed=4 * math.prod(shape), transcendentals=0),
        name=name,
    )(jnp.reshape(first, (1,)).astype(jnp.int32), source)


def cut_tokens_kernel(index, *refs):
    for i, source in enumerate(refs[:-1]):
        refs[-1][i] = source[...]


def cut_tokens(tokens, row_block, planes, rows):
    depth = tokens.shape[1] // planes

    def cut(i):
        return pl.BlockSpec((rows, depth), lambda n, index: (index[0], i))

    return pl.pallas_call(
        cut_tokens_kernel,
        out_shape=jax.ShapeDtypeStruct((planes, rows, depth), tokens.dtype),
        grid_spec=pltpu.PrefetchScalarGridSpec(
            num_scalar_prefetch=1,
            grid=(1,),
            in_specs=[cut(i) for i in range(planes)],
            out_specs=pl.BlockSpec((planes, rows, depth), lambda n, index: (0, 0, 0)),
        ),
        compiler_params=pltpu.CompilerParams(vmem_limit_bytes=48 * 1024 * 1024),
        cost_estimate=pl.CostEstimate(flops=0, bytes_accessed=4 * planes * rows * depth, transcendentals=0),
        name="cut_tokens",
    )(jnp.reshape(row_block, (1,)).astype(jnp.int32), *([tokens] * planes))


def cut_weight(weight, column_block, width, first_branch=0, branches=3):
    rows = weight.shape[1]
    if width % 128:
        cut = lax.dynamic_slice(weight, (first_branch, 0, column_block * width), (branches, rows, width))
        return jnp.transpose(cut, (1, 0, 2)).reshape(rows, branches * width)

    def cut(i):
        return (
            lambda source, first: source.at[first_branch + i, :, pl.ds(pl.multiple_of(first * width, width), width)],
            lambda target: target.at[:, pl.ds(i * width, width)],
        )

    return copy_cuts("cut_weight", [cut(i) for i in range(branches)], (rows, branches * width), column_block, weight)


def chain_kernel(slots, planes, has_got, place, *refs):
    terms, refs = refs[: len(slots)], refs[len(slots) :]
    got, refs = (refs[0], refs[1:]) if has_got else (None, refs)
    held, sem = refs[-2:]
    total = refs[-3] if slots[-1] == planes - 1 else None
    sent = refs[-4 if total is not None else -3] if slots[0] < planes - 1 else None
    for slot, term in zip(slots, terms):

        @pl.when(place[0] == slot)
        def _(slot=slot, term=term):
            copy = pltpu.make_async_copy(term, held, sem)
            copy.start()
            copy.wait()
            value = held[...]
            if has_got:
                value = value + got[...].astype(jnp.float32)
            if slot == planes - 1:
                total[...] = value
            else:
                sent[...] = value.astype(sent.dtype)


def run_chain(place, slots, planes, terms, got, total):
    rows, width3 = terms[0].shape
    outs, aliases = [], {}
    inputs = [place, *terms] + ([got] if got is not None else [])
    if slots[0] < planes - 1:
        outs.append(jax.ShapeDtypeStruct((rows, width3), jnp.bfloat16))
    if slots[-1] == planes - 1:
        if total is not None:
            aliases = {len(inputs): len(outs)}
            inputs.append(total)
        outs.append(jax.ShapeDtypeStruct((rows, width3), jnp.float32))
    vmem = pl.BlockSpec(memory_space=pltpu.VMEM)
    specs = [pl.BlockSpec(memory_space=pltpu.SMEM)] + [pl.BlockSpec(memory_space=pl.ANY)] * len(terms)
    result = pl.pallas_call(
        functools.partial(chain_kernel, tuple(slots), planes, got is not None),
        out_shape=outs,
        in_specs=specs + [vmem] * (len(inputs) - len(specs)),
        out_specs=[vmem] * len(outs),
        scratch_shapes=[pltpu.VMEM((rows, width3), jnp.float32), pltpu.SemaphoreType.DMA],
        input_output_aliases=aliases,
        compiler_params=pltpu.CompilerParams(vmem_limit_bytes=16 * 1024 * 1024),
        cost_estimate=pl.CostEstimate(flops=rows * width3, bytes_accessed=8 * rows * width3, transcendentals=0),
        name="chain",
    )(*inputs)
    sent = result[0] if slots[0] < planes - 1 else None
    return sent, (result[-1] if slots[-1] == planes - 1 else None)


def join_kernel(first, second, out):
    half = first.shape[2]
    out[:, :half] = first[0]
    out[:, half:] = second[0]


def join(first, second, order):
    blocks, rows, half = first.shape
    if half % 128:
        both = jnp.stack([first, second]).reshape((2,) + order + (rows, half))
        return both.transpose(4, 2, 3, 1, 0, 5).reshape(rows, -1)
    xs, ys, cs = order

    def source(i):
        return (i % xs) * ys * cs + i // xs

    return pl.pallas_call(
        join_kernel,
        out_shape=jax.ShapeDtypeStruct((rows, 2 * blocks * half), first.dtype),
        grid=(blocks,),
        in_specs=[pl.BlockSpec((1, rows, half), lambda i: (source(i), 0, 0))] * 2,
        out_specs=pl.BlockSpec((rows, 2 * half), lambda i: (0, i)),
        compiler_params=pltpu.CompilerParams(vmem_limit_bytes=8 * 1024 * 1024),
        name="join",
    )(first, second)


def after(value, *others):
    return lax.optimization_barrier((value, *others))[0]


def ring(axis, k):
    count = lax.axis_size(axis)
    return [(s, (s + k) % count) for s in range(count)]


def gather_rel(value, axis):
    count = lax.axis_size(axis)
    pieces = [value] + [lax.ppermute(value, axis, ring(axis, k)) for k in range(1, count)]
    return jnp.concatenate(pieces, axis=0) if count > 1 else value


def shards(tokens, in_weight, short_taps, decay_rates, residues):
    Z, X, Y, C = (lax.axis_size(a) for a in ("z", "x", "y", "c"))
    z, x, y, c = (lax.axis_index(a) for a in ("z", "x", "y", "c"))
    tok_rows, depth = tokens.shape
    w_rows, _, chans = in_weight.shape
    own = chans // X
    half = own // 2
    plane_depth = X * w_rows

    lower = z < Z // 2
    far_block = jnp.where(lower, 0, 1)
    near_block = 1 - far_block

    weight = jnp.transpose(in_weight, (1, 0, 2))

    def sends(block, *branches):
        return [cut_weight(weight, 2 * ((x + k) % X) + block, half, *branches) for k in range(1, X)]

    def moved(pieces):
        return [lax.ppermute(p, "x", ring("x", k + 1)) for k, p in enumerate(pieces)]

    def assemble(block, pieces):
        held = [cut_weight(weight, 2 * x + block, half)] + pieces
        rows = []
        for i in range(X):
            row = held[0]
            for k in range(1, X):
                row = jnp.where((x - i) % X == k, held[k], row)
            rows.append(row)
        return jnp.concatenate(rows, axis=0)

    share = tok_rows // (Y * C)
    part = share // 2
    far_sends = sends(far_block)
    far_got = moved(far_sends)
    mine = [cut_tokens(after(tokens, *far_sends), (y * C + c) * 2 + s, Z, part) for s in range(2)]

    def exchange(value):
        return lax.all_to_all(value, "z", split_axis=0, concat_axis=0, tiled=True)

    first = exchange(mine[0])
    second = exchange(after(mine[1], first))

    def both(k):
        return jnp.concatenate([first[k], second[k]], axis=0)

    def halves(split):
        return jnp.concatenate([split[0], split[1]], axis=0)

    near_sends = [sends(near_block, 0, 1), sends(near_block, 1, 2)]
    near_got = [None, None]
    near_weight = None
    far_weight = assemble(far_block, far_got)
    pairs, blocks = [], []
    last = None

    def add_group(k, *before):
        nonlocal near_weight, last
        if k == 0:
            pairs.append(gather_rel(after(halves(first), *far_got), "x"))
            near_got[0] = moved([after(p, pairs[0]) for p in near_sends[0]])
        elif k == 1:
            pairs.append(gather_rel(after(halves(second), *near_got[0], *before), "x"))
            near_got[1] = moved([after(p, pairs[1]) for p in near_sends[1]])
            near_weight = assemble(near_block, [jnp.concatenate(p, axis=1) for p in zip(*near_got)])
        else:
            pairs.append(gather_rel(after(both(k), *(near_got[1] if k == 2 else pairs[-1:]), *before), "x"))
        value = pairs[k]
        if last is not None:
            value = after(value, last)
        column = [value] + [lax.ppermute(value, "y", ring("y", j)) for j in range(1, Y)]
        last = column[-1]
        for value in column:
            blocks.append(value)
            blocks.extend(lax.ppermute(value, "c", ring("c", j)) for j in range(1, C))

    def places(*sizes):
        grids = jnp.meshgrid(*(jnp.arange(n, dtype=jnp.int32) for n in sizes), indexing="ij")
        return [g.reshape(-1) for g in grids]

    block_rows = X * share
    bz, bx, by, bc, bs = places(2, X, Y, C, 2)
    first_rows = ((bs * Y + (y - by) % Y) * C + (c - bc) % C) * block_rows + (((x - bx) % X) * 2 + bz) * part
    bx, by, bc = places(X, Y, C)
    other_rows = (((y - by) % Y) * C + (c - bc) % C) * block_rows + ((x - bx) % X) * share

    def near_cut(value):
        return lax.dynamic_slice_in_dim(value, x * own + near_block * half, half, axis=value.ndim - 1)

    taps = near_cut(short_taps).reshape(3, 3 * half)
    decay = near_cut(jnp.exp(-decay_rates))
    scaled = near_cut(residues * jnp.sqrt(2.0 * decay_rates))

    group_rows = block_rows * Y * C
    unit_rows = group_rows * Z // 8
    count = group_rows * Z // unit_rows
    place_up = jnp.reshape(z, (1,)).astype(jnp.int32)
    place_down = Z - 1 - place_up
    far, near = {}, {}
    ups, downs = {}, {}
    totals = []
    state = jnp.zeros_like(decay)
    halo = jnp.zeros((8, 3 * half), jnp.float32)
    outs = []
    before = []
    sent_ups = []

    def unit(u):
        while len(blocks) * block_rows < (u + 1) * unit_rows:
            k = len(pairs)
            add_group(k, *sent_ups[k - 1 : k])
        rows, start = [], u * unit_rows
        while start < (u + 1) * unit_rows:
            b, r = divmod(start, block_rows)
            stop = min(block_rows, r + (u + 1) * unit_rows - start)
            rows.append(blocks[b][r:stop])
            start += stop - r
        return jnp.concatenate(rows, axis=0)

    def emit(rows, piece, units):
        nonlocal state, halo
        out, state, halo = run_conv(
            rows % unit_rows // piece, rows // unit_rows, units, piece, taps, decay, scaled, state, halo
        )
        outs.append(out.reshape(X * Y * C, share, half))
        return [out]

    for tick in range(count + 2 * (Z - 1)):
        slots = [s for s in range(Z) if 0 <= tick - 2 * s < count]
        if tick < count:
            value = unit(tick)
            far[tick] = jnp.dot(value, far_weight, preferred_element_type=jnp.float32)
            near[tick] = value
        u = tick - 2 * (Z // 2)
        if 0 <= u < count:
            near[u] = jnp.dot(near[u], near_weight, preferred_element_type=jnp.float32)
        terms = [(far if s < Z // 2 else near)[tick - 2 * s] for s in slots]
        sent_up, total = run_chain(after(place_up, *before), slots, Z, terms, ups.get(tick - 2), None)
        if sent_up is not None:
            ups[tick] = lax.ppermute(sent_up, "z", [(s, s + 1) for s in slots if s + 1 < Z])
            sent_ups.append(sent_up)
        before = [total if sent_up is None else sent_up]
        sent_down, total = run_chain(after(place_down, *before), slots, Z, terms, downs.get(tick - 2), total)
        if sent_down is not None:
            downs[tick] = lax.ppermute(sent_down, "z", [(Z - 1 - s, Z - 2 - s) for s in slots if s + 1 < Z])
        before = [total if sent_down is None else sent_down]
        if total is not None:
            totals.append(total)
            have = len(totals) * unit_rows
            if len(outs) == 1:
                before += emit(first_rows[first_rows.shape[0] // 2 :], part, totals[: -(-2 * group_rows // unit_rows)])
            elif not outs and have >= 2 * group_rows:
                before += emit(first_rows[: first_rows.shape[0] // 2], part, totals)
            while len(outs) >= 2 and have >= (len(outs) + 1) * group_rows:
                start = len(outs) * group_rows
                begin, end = start // unit_rows, -(-(start + group_rows) // unit_rows)
                before += emit(other_rows + (start - begin * unit_rows), share, totals[begin:end])
    if len(outs) == 1:
        emit(first_rows[first_rows.shape[0] // 2 :], part, totals)

    def collect(home):
        total = jnp.where(z == home, outs[home], jnp.zeros_like(outs[home]))
        for k in range(Z):
            if k != home:
                total = total + lax.ppermute(outs[k], "z", [(home, k)])
        return total

    def spread(total):
        return lax.all_to_all(total, ("x", "y", "c"), split_axis=0, concat_axis=0, tiled=True)

    return join(spread(collect(Z - 1)), spread(collect(0)), (X, Y, C))


def solution(mesh):
    ctx, ch = mesh.shape["ctx"], mesh.shape["ch"]
    xs = 1
    while 4 * xs * xs <= ctx:
        xs *= 2
    cs = 2 if ch % 2 == 0 else 1
    fine = Mesh(mesh.devices.reshape(ctx // xs, xs, ch // cs, cs), ("z", "x", "y", "c"))
    return jax.shard_map(
        shards,
        mesh=fine,
        in_specs=(
            P(("z", "x"), None),
            P(("z", "x"), None, ("y", "c")),
            P(None, None, ("y", "c")),
            P(None, ("y", "c")),
            P(None, ("y", "c")),
        ),
        out_specs=P(("z", "x", "y", "c"), None),
        check_vma=False,
    )
```

```python
import functools

import jax
import jax.numpy as jnp
from jax import lax
from jax.experimental import pallas as pl
from jax.experimental.pallas import tpu as pltpu
from jax.sharding import Mesh
from jax.sharding import PartitionSpec as P


def conv_kernel(order, pick, *refs):
    parts = refs[:-11]
    taps, decay, scaled, state_in, halo_in, out, state, halo, ext, prod, modes = refs[-11:]
    rows, width = out.shape[1], out.shape[2]
    mode_count = decay.shape[0]
    tiles, _, lane = modes.shape
    i = pl.program_id(0)

    @pl.when(i == 0)
    def _():
        state[...] = state_in[...]
        halo[...] = halo_in[...]

    ext[0:8, :] = halo[...]
    for p, value in enumerate(parts):

        @pl.when(pick[i] == p)
        def _(value=value):
            ext[8 : 8 + rows, :] = value[0]

    halo[...] = ext[rows : rows + 8, :]

    def branch(i):
        cols = slice(i * width, (i + 1) * width)
        return (
            taps[0:1, cols] * ext[8 : 8 + rows, cols]
            + taps[1:2, cols] * ext[7 : 7 + rows, cols]
            + taps[2:3, cols] * ext[6 : 6 + rows, cols]
        )

    prod[...] = branch(1) * branch(2)
    halves = [slice(s, s + 8) for s in range(0, mode_count, 8)]
    decays = [decay[h, :] for h in halves]
    scales = [scaled[h, :] for h in halves]

    def step(t, states):
        entry = jnp.broadcast_to(prod[pl.ds(t, 1), :], (8, width))
        states = tuple(d * s + entry for d, s in zip(decays, states))
        total = scales[0] * states[0]
        for c, s in zip(scales[1:], states[1:]):
            total = total + c * s
        for i in range(tiles):
            modes[i, pl.ds(pl.multiple_of(t * 8, 8), 8), :] = total[:, i * lane : (i + 1) * lane]
        return states

    states = lax.fori_loop(0, rows, step, tuple(state[h, :] for h in halves), unroll=8)
    for h, s in zip(halves, states):
        state[h, :] = s
    gate = branch(0)
    for i in range(tiles):
        cols = slice(i * lane, (i + 1) * lane)
        conv = modes[i, pl.ds(0, rows, stride=8), :]
        for s in range(1, 8):
            conv = conv + modes[i, pl.ds(s, rows, stride=8), :]
        out[0, :, cols] = (gate[:, cols] * conv).astype(out.dtype)


def run_conv(order, pick, parts, rows, taps, decay, scaled, state, halo):
    blocks = order.shape[0]
    width3 = taps.shape[1]
    width = width3 // 3
    mode_count = decay.shape[0]
    lane = min(128, width)

    def whole(shape):
        return pl.BlockSpec(shape, lambda i, order, pick: (0,) * len(shape))

    return pl.pallas_call(
        conv_kernel,
        out_shape=(
            jax.ShapeDtypeStruct((blocks, rows, width), jnp.bfloat16),
            jax.ShapeDtypeStruct((mode_count, width), jnp.float32),
            jax.ShapeDtypeStruct((8, width3), jnp.float32),
        ),
        grid_spec=pltpu.PrefetchScalarGridSpec(
            num_scalar_prefetch=2,
            grid=(blocks,),
            in_specs=[pl.BlockSpec((1, rows, width3), lambda i, order, pick: (order[i], 0, 0))] * len(parts)
            + [
                whole((3, width3)),
                whole((mode_count, width)),
                whole((mode_count, width)),
                whole((mode_count, width)),
                whole((8, width3)),
            ],
            out_specs=[
                pl.BlockSpec((1, rows, width), lambda i, order, pick: (i, 0, 0)),
                whole((mode_count, width)),
                whole((8, width3)),
            ],
            scratch_shapes=[
                pltpu.VMEM((rows + 8, width3), jnp.float32),
                pltpu.VMEM((rows, width), jnp.float32),
                pltpu.VMEM((width // lane, rows * 8, lane), jnp.float32),
            ],
        ),
        compiler_params=pltpu.CompilerParams(vmem_limit_bytes=24 * 1024 * 1024),
        cost_estimate=pl.CostEstimate(flops=0, bytes_accessed=0, transcendentals=0),
        name="conv",
    )(order, pick, *(p.reshape(-1, rows, width3) for p in parts), taps, decay, scaled, state, halo)


def cut_tokens_kernel(index, *refs):
    for i, source in enumerate(refs[:-1]):
        refs[-1][i] = source[...]


def cut_tokens(tokens, row_block, planes, rows):
    depth = tokens.shape[1] // planes

    def cut(i):
        return pl.BlockSpec((rows, depth), lambda n, index: (index[0], i))

    return pl.pallas_call(
        cut_tokens_kernel,
        out_shape=jax.ShapeDtypeStruct((planes, rows, depth), tokens.dtype),
        grid_spec=pltpu.PrefetchScalarGridSpec(
            num_scalar_prefetch=1,
            grid=(1,),
            in_specs=[cut(i) for i in range(planes)],
            out_specs=pl.BlockSpec((planes, rows, depth), lambda n, index: (0, 0, 0)),
        ),
        compiler_params=pltpu.CompilerParams(vmem_limit_bytes=48 * 1024 * 1024),
        cost_estimate=pl.CostEstimate(flops=0, bytes_accessed=0, transcendentals=0),
        name="cut_tokens",
    )(jnp.reshape(row_block, (1,)).astype(jnp.int32), *([tokens] * planes))


def cut_weight_kernel(index, *refs):
    width = refs[0].shape[2]
    for i, source in enumerate(refs[:-1]):
        refs[-1][:, i * width : (i + 1) * width] = source[0]


def cut_weight(weight, column_block, width, first_branch=0, branches=3):
    rows = weight.shape[1]
    if width % 128:
        cut = lax.dynamic_slice(weight, (first_branch, 0, column_block * width), (branches, rows, width))
        return jnp.transpose(cut, (1, 0, 2)).reshape(rows, branches * width)

    def cut(i):
        return pl.BlockSpec((1, rows, width), lambda n, index: (first_branch + i, 0, index[0]))

    return pl.pallas_call(
        cut_weight_kernel,
        out_shape=jax.ShapeDtypeStruct((rows, branches * width), weight.dtype),
        grid_spec=pltpu.PrefetchScalarGridSpec(
            num_scalar_prefetch=1,
            grid=(1,),
            in_specs=[cut(i) for i in range(branches)],
            out_specs=pl.BlockSpec((rows, branches * width), lambda n, index: (0, 0)),
        ),
        compiler_params=pltpu.CompilerParams(vmem_limit_bytes=48 * 1024 * 1024),
        cost_estimate=pl.CostEstimate(flops=0, bytes_accessed=0, transcendentals=0),
        name="cut_weight",
    )(jnp.reshape(column_block, (1,)).astype(jnp.int32), *([weight] * branches))


def chain_kernel(slots, planes, has_got, place, *refs):
    terms, refs = refs[: len(slots)], refs[len(slots) :]
    got, refs = (refs[0], refs[1:]) if has_got else (None, refs)
    held, sem = refs[-2:]
    total = refs[-3] if slots[-1] == planes - 1 else None
    sent = refs[-4 if total is not None else -3] if slots[0] < planes - 1 else None
    for slot, term in zip(slots, terms):

        @pl.when(place[0] == slot)
        def _(slot=slot, term=term):
            copy = pltpu.make_async_copy(term, held, sem)
            copy.start()
            copy.wait()
            value = held[...]
            if has_got:
                value = value + got[...].astype(jnp.float32)
            if slot == planes - 1:
                total[...] = value
            else:
                sent[...] = value.astype(sent.dtype)


def run_chain(place, slots, planes, terms, got, total):
    rows, width3 = terms[0].shape
    outs, aliases = [], {}
    inputs = [place, *terms] + ([got] if got is not None else [])
    if slots[0] < planes - 1:
        outs.append(jax.ShapeDtypeStruct((rows, width3), jnp.bfloat16))
    if slots[-1] == planes - 1:
        if total is not None:
            aliases = {len(inputs): len(outs)}
            inputs.append(total)
        outs.append(jax.ShapeDtypeStruct((rows, width3), jnp.float32))
    vmem = pl.BlockSpec(memory_space=pltpu.VMEM)
    specs = [pl.BlockSpec(memory_space=pltpu.SMEM)] + [pl.BlockSpec(memory_space=pl.ANY)] * len(terms)
    result = pl.pallas_call(
        functools.partial(chain_kernel, tuple(slots), planes, got is not None),
        out_shape=outs,
        in_specs=specs + [vmem] * (len(inputs) - len(specs)),
        out_specs=[vmem] * len(outs),
        scratch_shapes=[pltpu.VMEM((rows, width3), jnp.float32), pltpu.SemaphoreType.DMA],
        input_output_aliases=aliases,
        compiler_params=pltpu.CompilerParams(vmem_limit_bytes=16 * 1024 * 1024),
        cost_estimate=pl.CostEstimate(flops=0, bytes_accessed=0, transcendentals=0),
        name="chain",
    )(*inputs)
    sent = result[0] if slots[0] < planes - 1 else None
    return sent, (result[-1] if slots[-1] == planes - 1 else None)


def term_kernel(*refs):
    blocks, weight, out = refs[:-2], refs[-2], refs[-1]
    row = 0
    for block in blocks:
        rows = block.shape[0]
        out[row : row + rows, :] = jnp.dot(block[...], weight[...], preferred_element_type=jnp.float32)
        row += rows


def term(blocks, weight):
    depth, width = weight.shape
    rows = sum(b.shape[0] for b in blocks)
    step = width // 3 if width // 3 % 128 == 0 else width
    return pl.pallas_call(
        term_kernel,
        out_shape=jax.ShapeDtypeStruct((rows, width), jnp.float32),
        grid=(width // step,),
        in_specs=[pl.BlockSpec(b.shape, lambda n: (0, 0)) for b in blocks]
        + [pl.BlockSpec((depth, step), lambda n: (0, n))],
        out_specs=pl.BlockSpec((rows, step), lambda n: (0, n)),
        compiler_params=pltpu.CompilerParams(vmem_limit_bytes=32 * 1024 * 1024),
        cost_estimate=pl.CostEstimate(flops=0, bytes_accessed=0, transcendentals=0),
        name="term",
    )(*blocks, weight)


def join_kernel(first, second, out):
    half = first.shape[2]
    out[:, :half] = first[0]
    out[:, half:] = second[0]


def join(first, second, order):
    blocks, rows, half = first.shape
    if half % 128:
        both = jnp.stack([first, second]).reshape((2,) + order + (rows, half))
        return both.transpose(4, 2, 3, 1, 0, 5).reshape(rows, -1)
    xs, ys, cs = order

    def source(i):
        return (i % xs) * ys * cs + i // xs

    return pl.pallas_call(
        join_kernel,
        out_shape=jax.ShapeDtypeStruct((rows, 2 * blocks * half), first.dtype),
        grid=(blocks,),
        in_specs=[pl.BlockSpec((1, rows, half), lambda i: (source(i), 0, 0))] * 2,
        out_specs=pl.BlockSpec((rows, 2 * half), lambda i: (0, i)),
        compiler_params=pltpu.CompilerParams(vmem_limit_bytes=8 * 1024 * 1024),
        name="join",
    )(first, second)


def after(value, *others):
    return lax.optimization_barrier((value, *others))[0]


def ring(axis, k):
    count = lax.axis_size(axis)
    return [(s, (s + k) % count) for s in range(count)]


def gather_rel(value, axis):
    count = lax.axis_size(axis)
    pieces = [value] + [lax.ppermute(value, axis, ring(axis, k)) for k in range(1, count)]
    return jnp.concatenate(pieces, axis=0) if count > 1 else value


def shards(tokens, in_weight, short_taps, decay_rates, residues):
    Z, X, Y, C = (lax.axis_size(a) for a in ("z", "x", "y", "c"))
    z, x, y, c = (lax.axis_index(a) for a in ("z", "x", "y", "c"))
    tok_rows, depth = tokens.shape
    w_rows, _, chans = in_weight.shape
    own = chans // X
    half = own // 2
    plane_depth = X * w_rows

    lower = z < Z // 2
    far_block = jnp.where(lower, 0, 1)
    near_block = 1 - far_block

    weight = jnp.transpose(in_weight, (1, 0, 2))

    def sends(block, *branches):
        return [cut_weight(weight, 2 * ((x + k) % X) + block, half, *branches) for k in range(1, X)]

    def moved(pieces):
        return [lax.ppermute(p, "x", ring("x", k + 1)) for k, p in enumerate(pieces)]

    def assemble(kept, pieces):
        held = [kept] + pieces
        rows = []
        for i in range(X):
            row = held[0]
            for k in range(1, X):
                row = jnp.where((x - i) % X == k, held[k], row)
            rows.append(row)
        return jnp.concatenate(rows, axis=0)

    share = tok_rows // (Y * C)
    far_sends = sends(far_block)
    far_got = moved(far_sends)
    mine = cut_tokens(after(tokens, *far_sends), y * C + c, Z, share)
    split = lax.all_to_all(mine, "z", split_axis=0, concat_axis=0, tiled=True)
    near_sends = [sends(near_block, 0, 1), sends(near_block, 1, 2)]
    near_got = [moved([after(p, *far_got) for p in near_sends[0]]), None]
    kept = [cut_weight(weight, 2 * x + block, half) for block in (far_block, near_block)]
    split = list(after(split, *near_got[0], *near_sends[1], *kept))
    far_weight = assemble(kept[0], far_got)
    near_weight = None

    pairs, others = [], []
    sent_ups = []

    def first_step(k, *before):
        pairs.append(gather_rel(after(split[k], *before), "xy"[k % 2]))

    def second_step(k, *before):
        axis = "yx"[k % 2]
        value = after(pairs[k], *before)
        others.append([lax.ppermute(value, axis, ring(axis, j)) for j in range(1, lax.axis_size(axis))])

    def add_planes(k):
        planes = range(k, min(k + 2, Z))
        for i in planes:
            first_step(i, *sent_ups[max(0, k - 2) : k - 1])
        for i in planes:
            second_step(i, *(sent_ups[k - 1 + i % 2 : k + i % 2] if k else []))

    def places(*sizes):
        grids = jnp.meshgrid(*(jnp.arange(n, dtype=jnp.int32) for n in sizes), indexing="ij")
        return [g.reshape(-1) for g in grids]

    bx, by, bc = places(X, Y, C)
    rel_x, rel_y, rel_c = (x - bx) % X, (y - by) % Y, (c - bc) % C
    group_rows = X * Y * C * share
    lead = [C * (X, Y)[k % 2] * share for k in range(Z)]

    def rows_of(k):
        column, inner = (rel_y, rel_x) if k % 2 == 0 else (rel_x, rel_y)
        head, tail = k * group_rows, k * group_rows + lead[k]
        if k < 2:
            head, tail = (0, lead[0] + lead[1]) if k == 0 else (lead[0], group_rows + lead[1])
        place = jnp.where(column == 0, head, tail + (column - 1) * lead[k])
        return place + rel_c * (lead[k] // C) + inner * share

    def near_cut(value):
        return lax.dynamic_slice_in_dim(value, x * own + near_block * half, half, axis=value.ndim - 1)

    taps = near_cut(short_taps).reshape(3, 3 * half)
    decay = near_cut(jnp.exp(-decay_rates))
    scaled = near_cut(residues * jnp.sqrt(2.0 * decay_rates))

    unit_rows = group_rows * Z // 8
    count = group_rows * Z // unit_rows
    place_up = jnp.reshape(z, (1,)).astype(jnp.int32)
    place_down = Z - 1 - place_up
    far, near = {}, {}
    ups, downs = {}, {}
    totals = []
    state = jnp.zeros_like(decay)
    halo = jnp.zeros((8, 3 * half), jnp.float32)
    outs = []
    before = []
    came, due = {}, {}

    blocks, columns, used = [], [], list(range(Z))
    add_planes(0)

    def unit(u):
        nonlocal blocks
        rows, have = [], 0
        while have < unit_rows:
            if not blocks:
                if not columns:
                    k = used.pop(0)
                    while len(pairs) <= k:
                        add_planes(len(pairs))
                    if k == 0:
                        columns.extend(pairs[:2] + others[0] + others[1])
                        used.pop(0)
                    else:
                        columns.extend([pairs[k]] + others[k])
                value = columns.pop(0)
                blocks = [value]
                if u > 0:
                    value = after(value, sent_ups[max(0, u - 2)])
                blocks += [lax.ppermute(value, "c", ring("c", j)) for j in range(1, C)]
            block = blocks.pop(0)
            if block.shape[0] > unit_rows - have:
                blocks.insert(0, block[unit_rows - have :])
                block = block[: unit_rows - have]
            rows.append(block)
            have += block.shape[0]
        rows[0] = after(rows[0], *sent_ups[u - 1 : u])
        return rows

    def ready(plane):
        return group_rows + lead[1] if plane == 0 else (plane + 1) * group_rows

    def emit(plane):
        nonlocal state, halo
        first = 0 if plane < 2 else plane * group_rows
        begin, end = first // unit_rows, -(-ready(plane) // unit_rows)
        rows = rows_of(plane) - begin * unit_rows
        out, state, halo = run_conv(
            rows % unit_rows // share, rows // unit_rows, totals[begin:end], share, taps, decay, scaled, state, halo
        )
        outs.append(out.reshape(X * Y * C, share, half))
        return out

    for tick in range(count + 2 * (Z - 1)):
        slots = [s for s in range(Z) if 0 <= tick - 2 * s < count]
        if tick < count:
            value = unit(tick)
            far[tick] = term(value, far_weight)
            near[tick] = value
        u = tick - 2 * (Z // 2)
        if 0 <= u < count:
            if near_weight is None:
                near_got[1] = moved([after(p, *sent_ups[1:2]) for p in near_sends[1]])
                whole = [jnp.concatenate(p, axis=1) for p in zip(*near_got)]
                near_weight = assemble(kept[1], [after(p, *sent_ups[tick - 1 : tick]) for p in whole])
            value = after(near[u][0], *(sent_ups[tick - 1 : tick] or before))
            near[u] = term([value] + near[u][1:], near_weight)
        terms = [(far if s < Z // 2 else near)[tick - 2 * s] for s in slots]
        sent_up, total = run_chain(after(place_up, *before), slots, Z, terms, ups.get(tick - 2), None)
        if sent_up is not None:
            ups[tick] = lax.ppermute(sent_up, "z", [(s, s + 1) for s in slots if s + 1 < Z])
            sent_ups.append(sent_up)
        before = [total if sent_up is None else sent_up]
        sent_down, total = run_chain(after(place_down, *before), slots, Z, terms, downs.get(tick - 2), total)
        if sent_down is not None:
            downs[tick] = lax.ppermute(sent_down, "z", [(Z - 1 - s, Z - 2 - s) for s in slots if s + 1 < Z])
        before = [total if sent_down is None else sent_down] + due.pop(tick + 1, [])
        if total is not None:
            totals.append(total)
            if len(outs) < Z and len(totals) * unit_rows >= ready(len(outs)):
                k = len(outs)
                before.append(emit(k))
                for home in (0, Z - 1):
                    if 0 < abs(k - home) < Z - 1 and tick + 3 < count + 2 * (Z - 1):
                        came[home, k] = lax.ppermute(outs[k], "z", [(home, k)])
                        due.setdefault(count + 2 * (Z - 1) - 1, []).append(came[home, k])
    while len(outs) < Z:
        emit(len(outs))

    def collect(home):
        total = jnp.where(z == home, outs[home], jnp.zeros_like(outs[home]))
        for k in range(Z):
            if k != home:
                if (home, k) not in came:
                    value = after(outs[k], totals[-1]) if k == 0 else outs[k]
                    came[home, k] = lax.ppermute(value, "z", [(home, k)])
                total = total + came[home, k]
        return total

    def spread(total):
        return lax.all_to_all(total, ("x", "y", "c"), split_axis=0, concat_axis=0, tiled=True)

    return join(spread(collect(Z - 1)), spread(collect(0)), (X, Y, C))


def solution(mesh):
    ctx, ch = mesh.shape["ctx"], mesh.shape["ch"]
    xs = 1
    while 4 * xs * xs <= ctx:
        xs *= 2
    cs = 2 if ch % 2 == 0 else 1
    fine = Mesh(mesh.devices.reshape(ctx // xs, xs, ch // cs, cs), ("z", "x", "y", "c"))
    return jax.shard_map(
        shards,
        mesh=fine,
        in_specs=(
            P(("z", "x"), None),
            P(("z", "x"), None, ("y", "c")),
            P(None, None, ("y", "c")),
            P(None, ("y", "c")),
            P(None, ("y", "c")),
        ),
        out_specs=P(("z", "x", "y", "c"), None),
        check_vma=False,
    )
```

```python
import functools

import jax
import jax.numpy as jnp
from jax import lax
from jax.experimental import pallas as pl
from jax.experimental.pallas import tpu as pltpu
from jax.sharding import Mesh
from jax.sharding import PartitionSpec as P


def conv_kernel(order, pick, *refs):
    parts = refs[:-11]
    taps, decay, scaled, state_in, halo_in, out, state, halo, ext, prod, modes = refs[-11:]
    rows, width = out.shape[1], out.shape[2]
    mode_count = decay.shape[0]
    tiles, _, lane = modes.shape
    i = pl.program_id(0)

    @pl.when(i == 0)
    def _():
        state[...] = state_in[...]
        halo[...] = halo_in[...]

    ext[0:8, :] = halo[...]
    for p, value in enumerate(parts):

        @pl.when(pick[i] == p)
        def _(value=value):
            ext[8 : 8 + rows, :] = value[0]

    halo[...] = ext[rows : rows + 8, :]

    def branch(i):
        cols = slice(i * width, (i + 1) * width)
        return (
            taps[0:1, cols] * ext[8 : 8 + rows, cols]
            + taps[1:2, cols] * ext[7 : 7 + rows, cols]
            + taps[2:3, cols] * ext[6 : 6 + rows, cols]
        )

    prod[...] = branch(1) * branch(2)
    halves = [slice(s, s + 8) for s in range(0, mode_count, 8)]
    decays = [decay[h, :] for h in halves]
    scales = [scaled[h, :] for h in halves]

    def step(t, states):
        entry = jnp.broadcast_to(prod[pl.ds(t, 1), :], (8, width))
        states = tuple(d * s + entry for d, s in zip(decays, states))
        total = scales[0] * states[0]
        for c, s in zip(scales[1:], states[1:]):
            total = total + c * s
        for i in range(tiles):
            modes[i, pl.ds(pl.multiple_of(t * 8, 8), 8), :] = total[:, i * lane : (i + 1) * lane]
        return states

    states = lax.fori_loop(0, rows, step, tuple(state[h, :] for h in halves), unroll=8)
    for h, s in zip(halves, states):
        state[h, :] = s
    gate = branch(0)
    for i in range(tiles):
        cols = slice(i * lane, (i + 1) * lane)
        conv = modes[i, pl.ds(0, rows, stride=8), :]
        for s in range(1, 8):
            conv = conv + modes[i, pl.ds(s, rows, stride=8), :]
        out[0, :, cols] = (gate[:, cols] * conv).astype(out.dtype)


def run_conv(order, pick, parts, rows, taps, decay, scaled, state, halo):
    blocks = order.shape[0]
    width3 = taps.shape[1]
    width = width3 // 3
    mode_count = decay.shape[0]
    lane = min(128, width)

    def whole(shape):
        return pl.BlockSpec(shape, lambda i, order, pick: (0,) * len(shape))

    return pl.pallas_call(
        conv_kernel,
        out_shape=(
            jax.ShapeDtypeStruct((blocks, rows, width), jnp.bfloat16),
            jax.ShapeDtypeStruct((mode_count, width), jnp.float32),
            jax.ShapeDtypeStruct((8, width3), jnp.float32),
        ),
        grid_spec=pltpu.PrefetchScalarGridSpec(
            num_scalar_prefetch=2,
            grid=(blocks,),
            in_specs=[pl.BlockSpec((1, rows, width3), lambda i, order, pick: (order[i], 0, 0))] * len(parts)
            + [
                whole((3, width3)),
                whole((mode_count, width)),
                whole((mode_count, width)),
                whole((mode_count, width)),
                whole((8, width3)),
            ],
            out_specs=[
                pl.BlockSpec((1, rows, width), lambda i, order, pick: (i, 0, 0)),
                whole((mode_count, width)),
                whole((8, width3)),
            ],
            scratch_shapes=[
                pltpu.VMEM((rows + 8, width3), jnp.float32),
                pltpu.VMEM((rows, width), jnp.float32),
                pltpu.VMEM((width // lane, rows * 8, lane), jnp.float32),
            ],
        ),
        compiler_params=pltpu.CompilerParams(vmem_limit_bytes=16 * 1024 * 1024),
        cost_estimate=pl.CostEstimate(flops=0, bytes_accessed=0, transcendentals=0),
        name="conv",
    )(order, pick, *(p.reshape(-1, rows, width3) for p in parts), taps, decay, scaled, state, halo)


def cut_tokens_kernel(index, *refs):
    for i, source in enumerate(refs[:-1]):
        refs[-1][i] = source[...]


def cut_tokens(tokens, row_block, planes, rows):
    depth = tokens.shape[1] // planes

    def cut(i):
        return pl.BlockSpec((rows, depth), lambda n, index: (index[0], i))

    return pl.pallas_call(
        cut_tokens_kernel,
        out_shape=jax.ShapeDtypeStruct((planes, rows, depth), tokens.dtype),
        grid_spec=pltpu.PrefetchScalarGridSpec(
            num_scalar_prefetch=1,
            grid=(1,),
            in_specs=[cut(i) for i in range(planes)],
            out_specs=pl.BlockSpec((planes, rows, depth), lambda n, index: (0, 0, 0)),
        ),
        compiler_params=pltpu.CompilerParams(vmem_limit_bytes=48 * 1024 * 1024),
        cost_estimate=pl.CostEstimate(flops=0, bytes_accessed=0, transcendentals=0),
        name="cut_tokens",
    )(jnp.reshape(row_block, (1,)).astype(jnp.int32), *([tokens] * planes))


def cut_weight_kernel(index, *refs):
    width = refs[0].shape[2]
    for i, source in enumerate(refs[:-1]):
        refs[-1][:, i * width : (i + 1) * width] = source[0]


def cut_weight(weight, column_block, width, first_branch=0, branches=3):
    rows = weight.shape[1]
    if width % 128:
        cut = lax.dynamic_slice(weight, (first_branch, 0, column_block * width), (branches, rows, width))
        return jnp.transpose(cut, (1, 0, 2)).reshape(rows, branches * width)

    def cut(i):
        return pl.BlockSpec((1, rows, width), lambda n, index: (first_branch + i, 0, index[0]))

    return pl.pallas_call(
        cut_weight_kernel,
        out_shape=jax.ShapeDtypeStruct((rows, branches * width), weight.dtype),
        grid_spec=pltpu.PrefetchScalarGridSpec(
            num_scalar_prefetch=1,
            grid=(1,),
            in_specs=[cut(i) for i in range(branches)],
            out_specs=pl.BlockSpec((rows, branches * width), lambda n, index: (0, 0)),
        ),
        compiler_params=pltpu.CompilerParams(vmem_limit_bytes=48 * 1024 * 1024),
        cost_estimate=pl.CostEstimate(flops=0, bytes_accessed=0, transcendentals=0),
        name="cut_weight",
    )(jnp.reshape(column_block, (1,)).astype(jnp.int32), *([weight] * branches))


def chain_kernel(slots, planes, has_got, place, *refs):
    terms, refs = refs[: len(slots)], refs[len(slots) :]
    got, refs = (refs[0], refs[1:]) if has_got else (None, refs)
    held, sem = refs[-2:]
    total = refs[-3] if slots[-1] == planes - 1 else None
    sent = refs[-4 if total is not None else -3] if slots[0] < planes - 1 else None
    for slot, term in zip(slots, terms):

        @pl.when(place[0] == slot)
        def _(slot=slot, term=term):
            copy = pltpu.make_async_copy(term, held, sem)
            copy.start()
            copy.wait()
            value = held[...]
            if has_got:
                value = value + got[...].astype(jnp.float32)
            if slot == planes - 1:
                total[...] = value
            else:
                sent[...] = value.astype(sent.dtype)


def run_chain(place, slots, planes, terms, got, total):
    rows, width3 = terms[0].shape
    outs, aliases = [], {}
    inputs = [place, *terms] + ([got] if got is not None else [])
    if slots[0] < planes - 1:
        outs.append(jax.ShapeDtypeStruct((rows, width3), jnp.bfloat16))
    if slots[-1] == planes - 1:
        if total is not None:
            aliases = {len(inputs): len(outs)}
            inputs.append(total)
        outs.append(jax.ShapeDtypeStruct((rows, width3), jnp.float32))
    vmem = pl.BlockSpec(memory_space=pltpu.VMEM)
    specs = [pl.BlockSpec(memory_space=pltpu.SMEM)] + [pl.BlockSpec(memory_space=pl.ANY)] * len(terms)
    result = pl.pallas_call(
        functools.partial(chain_kernel, tuple(slots), planes, got is not None),
        out_shape=outs,
        in_specs=specs + [vmem] * (len(inputs) - len(specs)),
        out_specs=[vmem] * len(outs),
        scratch_shapes=[pltpu.VMEM((rows, width3), jnp.float32), pltpu.SemaphoreType.DMA],
        input_output_aliases=aliases,
        compiler_params=pltpu.CompilerParams(vmem_limit_bytes=8 * 1024 * 1024),
        cost_estimate=pl.CostEstimate(flops=0, bytes_accessed=0, transcendentals=0),
        name="chain",
    )(*inputs)
    sent = result[0] if slots[0] < planes - 1 else None
    return sent, (result[-1] if slots[-1] == planes - 1 else None)


def term_kernel(*refs):
    blocks, weight, out = refs[:-2], refs[-2], refs[-1]
    row = 0
    for block in blocks:
        rows = block.shape[0]
        out[row : row + rows, :] = jnp.dot(block[...], weight[...], preferred_element_type=jnp.float32)
        row += rows


def term(blocks, weight):
    depth, width = weight.shape
    rows = sum(b.shape[0] for b in blocks)
    step = width // 3 if width // 3 % 128 == 0 else width
    return pl.pallas_call(
        term_kernel,
        out_shape=jax.ShapeDtypeStruct((rows, width), jnp.float32),
        grid=(width // step,),
        in_specs=[pl.BlockSpec(b.shape, lambda n: (0, 0)) for b in blocks]
        + [pl.BlockSpec((depth, step), lambda n: (0, n))],
        out_specs=pl.BlockSpec((rows, step), lambda n: (0, n)),
        compiler_params=pltpu.CompilerParams(vmem_limit_bytes=16 * 1024 * 1024),
        cost_estimate=pl.CostEstimate(flops=0, bytes_accessed=0, transcendentals=0),
        name="term",
    )(*blocks, weight)


def join_kernel(first, second, out):
    half = first.shape[2]
    out[:, :half] = first[0]
    out[:, half:] = second[0]


def join(first, second, order):
    blocks, rows, half = first.shape
    if half % 128:
        both = jnp.stack([first, second]).reshape((2,) + order + (rows, half))
        return both.transpose(4, 2, 3, 1, 0, 5).reshape(rows, -1)
    xs, ys, cs = order

    def source(i):
        return (i % xs) * ys * cs + i // xs

    return pl.pallas_call(
        join_kernel,
        out_shape=jax.ShapeDtypeStruct((rows, 2 * blocks * half), first.dtype),
        grid=(blocks,),
        in_specs=[pl.BlockSpec((1, rows, half), lambda i: (source(i), 0, 0))] * 2,
        out_specs=pl.BlockSpec((rows, 2 * half), lambda i: (0, i)),
        compiler_params=pltpu.CompilerParams(vmem_limit_bytes=8 * 1024 * 1024),
        name="join",
    )(first, second)


def after(value, *others):
    return lax.optimization_barrier((value, *others))[0]


def ring(axis, k):
    count = lax.axis_size(axis)
    return [(s, (s + k) % count) for s in range(count)]


def gather_rel(value, axis):
    count = lax.axis_size(axis)
    pieces = [value] + [lax.ppermute(value, axis, ring(axis, k)) for k in range(1, count)]
    return jnp.concatenate(pieces, axis=0) if count > 1 else value


def shards(tokens, in_weight, short_taps, decay_rates, residues):
    Z, X, Y, C = (lax.axis_size(a) for a in ("z", "x", "y", "c"))
    z, x, y, c = (lax.axis_index(a) for a in ("z", "x", "y", "c"))
    tok_rows, depth = tokens.shape
    w_rows, _, chans = in_weight.shape
    own = chans // X
    half = own // 2
    plane_depth = X * w_rows

    lower = z < Z // 2
    far_block = jnp.where(lower, 0, 1)
    near_block = 1 - far_block

    weight = jnp.transpose(in_weight, (1, 0, 2))

    def sends(block, *branches):
        return [cut_weight(weight, 2 * ((x + k) % X) + block, half, *branches) for k in range(1, X)]

    def moved(pieces):
        return [lax.ppermute(p, "x", ring("x", k + 1)) for k, p in enumerate(pieces)]

    def assemble(kept, pieces):
        held = [kept] + pieces
        rows = []
        for i in range(X):
            row = held[0]
            for k in range(1, X):
                row = jnp.where((x - i) % X == k, held[k], row)
            rows.append(row)
        return jnp.concatenate(rows, axis=0)

    share = tok_rows // (Y * C)
    far_sends = sends(far_block)
    far_got = moved(far_sends)
    mine = cut_tokens(after(tokens, *far_sends), y * C + c, Z, share)
    split = lax.all_to_all(mine, "z", split_axis=0, concat_axis=0, tiled=True)
    near_sends = [sends(near_block, 0, 1), sends(near_block, 1, 2)]
    near_got = [moved([after(p, *far_got) for p in near_sends[0]]), None]
    kept = [cut_weight(weight, 2 * x + block, half) for block in (far_block, near_block)]
    def places(*sizes):
        grids = jnp.meshgrid(*(jnp.arange(n, dtype=jnp.int32) for n in sizes), indexing="ij")
        return [g.reshape(-1) for g in grids]

    bx, by, bc = places(X, Y, C)
    rel_x, rel_y, rel_c = (x - bx) % X, (y - by) % Y, (c - bc) % C
    group_rows = X * Y * C * share
    unit_rows = group_rows * Z // 8
    lead = [C * (X, Y)[k % 2] * share for k in range(Z)]

    def rows_of(k):
        column, inner = (rel_y, rel_x) if k % 2 == 0 else (rel_x, rel_y)
        head, tail = k * group_rows, k * group_rows + lead[k]
        if k < 2:
            head, tail = (0, lead[0] + lead[1]) if k == 0 else (lead[0], group_rows + lead[1])
        place = jnp.where(column == 0, head, tail + (column - 1) * lead[k])
        return place + rel_c * (lead[k] // C) + inner * share

    def near_cut(value):
        return lax.dynamic_slice_in_dim(value, x * own + near_block * half, half, axis=value.ndim - 1)

    taps = near_cut(short_taps).reshape(3, 3 * half)
    decay = near_cut(jnp.exp(-decay_rates))
    scaled = near_cut(residues * jnp.sqrt(2.0 * decay_rates))

    place_up = jnp.reshape(z, (1,)).astype(jnp.int32)
    place_down = Z - 1 - place_up
    orders = []
    for k in range(Z):
        first = 0 if k < 2 else k * group_rows // unit_rows
        rows = rows_of(k) - first * unit_rows
        orders.append((first, rows % unit_rows // share, rows // unit_rows))
    small = [taps, decay, scaled, place_up, place_down] + [v for o in orders for v in o[1:]]

    far_weight = assemble(kept[0], far_got)
    split = list(after(split, far_weight, *near_got[0], *near_sends[1], *kept, *small))
    near_weight = None

    pairs, others = [], []
    sent_ups = []

    def first_step(k, *before):
        pairs.append(gather_rel(after(split[k], *before), "xy"[k % 2]))

    def second_step(k, *before):
        axis = "yx"[k % 2]
        value = after(pairs[k], *before)
        others.append([lax.ppermute(value, axis, ring(axis, j)) for j in range(1, lax.axis_size(axis))])

    def add_planes(k):
        planes = range(k, min(k + 2, Z))
        for i in planes:
            first_step(i, *sent_ups[max(0, k - 2) : k - 1])
        if k == 0:
            pairs[:] = lax.optimization_barrier(tuple(pairs))
        for i in planes:
            second_step(i, *(sent_ups[k - 1 + i % 2 : k + i % 2] if k else []))

    count = group_rows * Z // unit_rows
    far, near = {}, {}
    ups, downs = {}, {}
    totals = []
    state = jnp.zeros_like(decay)
    halo = jnp.zeros((8, 3 * half), jnp.float32)
    outs = []
    before = []
    came, due = {}, {}

    blocks, columns, used = [], [], list(range(Z))
    add_planes(0)

    def unit(u):
        nonlocal blocks
        rows, have = [], 0
        while have < unit_rows:
            if not blocks:
                if not columns:
                    k = used.pop(0)
                    while len(pairs) <= k:
                        add_planes(len(pairs))
                    if k == 0:
                        columns.extend(pairs[:2] + others[0] + others[1])
                        used.pop(0)
                    else:
                        columns.extend([pairs[k]] + others[k])
                value = columns.pop(0)
                blocks = [value]
                if u > 0:
                    value = after(value, sent_ups[max(0, u - 2)])
                blocks += [lax.ppermute(value, "c", ring("c", j)) for j in range(1, C)]
            block = blocks.pop(0)
            if block.shape[0] > unit_rows - have:
                blocks.insert(0, block[unit_rows - have :])
                block = block[: unit_rows - have]
            rows.append(block)
            have += block.shape[0]
        rows[0] = after(rows[0], *sent_ups[u - 1 : u])
        return rows

    def ready(plane):
        return group_rows + lead[1] if plane == 0 else (plane + 1) * group_rows

    def emit(plane):
        nonlocal state, halo
        first, order, pick = orders[plane]
        parts = totals[first : -(-ready(plane) // unit_rows)]
        out, state, halo = run_conv(order, pick, parts, share, taps, decay, scaled, state, halo)
        outs.append(out.reshape(X * Y * C, share, half))
        return out

    for tick in range(count + 2 * (Z - 1)):
        slots = [s for s in range(Z) if 0 <= tick - 2 * s < count]
        if tick < count:
            value = unit(tick)
            far[tick] = term(value, far_weight)
            near[tick] = value
        u = tick - 2 * (Z // 2)
        if 0 <= u < count:
            if near_weight is None:
                near_got[1] = moved([after(p, *sent_ups[1:2]) for p in near_sends[1]])
                whole = [jnp.concatenate(p, axis=1) for p in zip(*near_got)]
                near_weight = assemble(kept[1], [after(p, *sent_ups[tick - 1 : tick]) for p in whole])
            value = after(near[u][0], *(sent_ups[tick - 1 : tick] or before))
            near[u] = term([value] + near[u][1:], near_weight)
        terms = [(far if s < Z // 2 else near)[tick - 2 * s] for s in slots]
        sent_up, total = run_chain(after(place_up, *before), slots, Z, terms, ups.get(tick - 2), None)
        if sent_up is not None:
            ups[tick] = lax.ppermute(sent_up, "z", [(s, s + 1) for s in slots if s + 1 < Z])
            sent_ups.append(sent_up)
        before = [total if sent_up is None else sent_up]
        sent_down, total = run_chain(after(place_down, *before), slots, Z, terms, downs.get(tick - 2), total)
        if sent_down is not None:
            downs[tick] = lax.ppermute(sent_down, "z", [(Z - 1 - s, Z - 2 - s) for s in slots if s + 1 < Z])
        before = [total if sent_down is None else sent_down] + due.pop(tick + 1, [])
        if total is not None:
            totals.append(total)
            if len(outs) < Z and len(totals) * unit_rows >= ready(len(outs)):
                k = len(outs)
                before.append(emit(k))
                for home in (0, Z - 1):
                    if 0 < abs(k - home) < Z - 1 and tick + 3 < count + 2 * (Z - 1):
                        came[home, k] = lax.ppermute(outs[k], "z", [(home, k)])
                        due.setdefault(count + 2 * (Z - 1) - 1, []).append(came[home, k])
    while len(outs) < Z:
        emit(len(outs))

    def collect(home):
        total = jnp.where(z == home, outs[home], jnp.zeros_like(outs[home]))
        for k in range(Z):
            if k != home:
                if (home, k) not in came:
                    value = after(outs[k], totals[-1]) if k == 0 else outs[k]
                    came[home, k] = lax.ppermute(value, "z", [(home, k)])
                total = total + came[home, k]
        return total

    def spread(total):
        return lax.all_to_all(total, ("x", "y", "c"), split_axis=0, concat_axis=0, tiled=True)

    upper = spread(collect(Z - 1))
    return join(upper, spread(after(collect(0), upper)), (X, Y, C))


def solution(mesh):
    ctx, ch = mesh.shape["ctx"], mesh.shape["ch"]
    xs = 1
    while 4 * xs * xs <= ctx:
        xs *= 2
    cs = 2 if ch % 2 == 0 else 1
    fine = Mesh(mesh.devices.reshape(ctx // xs, xs, ch // cs, cs), ("z", "x", "y", "c"))
    return jax.shard_map(
        shards,
        mesh=fine,
        in_specs=(
            P(("z", "x"), None),
            P(("z", "x"), None, ("y", "c")),
            P(None, None, ("y", "c")),
            P(None, ("y", "c")),
            P(None, ("y", "c")),
        ),
        out_specs=P(("z", "x", "y", "c"), None),
        check_vma=False,
    )
```

```python
import functools

import jax
import jax.numpy as jnp
from jax import lax
from jax.experimental import pallas as pl
from jax.experimental.pallas import tpu as pltpu
from jax.sharding import Mesh
from jax.sharding import PartitionSpec as P


def conv_kernel(order, pick, *refs):
    parts = refs[:-11]
    taps, decay, scaled, state_in, halo_in, out, state, halo, ext, prod, modes = refs[-11:]
    rows, width = out.shape[1], out.shape[2]
    mode_count = decay.shape[0]
    tiles, _, lane = modes.shape
    i = pl.program_id(0)

    @pl.when(i == 0)
    def _():
        state[...] = state_in[...]
        halo[...] = halo_in[...]

    ext[0:8, :] = halo[...]
    for p, value in enumerate(parts):

        @pl.when(pick[i] == p)
        def _(value=value):
            ext[8 : 8 + rows, :] = value[0]

    halo[...] = ext[rows : rows + 8, :]

    def branch(i):
        cols = slice(i * width, (i + 1) * width)
        return (
            taps[0:1, cols] * ext[8 : 8 + rows, cols]
            + taps[1:2, cols] * ext[7 : 7 + rows, cols]
            + taps[2:3, cols] * ext[6 : 6 + rows, cols]
        )

    prod[...] = branch(1) * branch(2)
    halves = [slice(s, s + 8) for s in range(0, mode_count, 8)]
    decays = [decay[h, :] for h in halves]
    scales = [scaled[h, :] for h in halves]

    def step(t, states):
        entry = jnp.broadcast_to(prod[pl.ds(t, 1), :], (8, width))
        states = tuple(d * s + entry for d, s in zip(decays, states))
        total = scales[0] * states[0]
        for c, s in zip(scales[1:], states[1:]):
            total = total + c * s
        for i in range(tiles):
            modes[i, pl.ds(pl.multiple_of(t * 8, 8), 8), :] = total[:, i * lane : (i + 1) * lane]
        return states

    states = lax.fori_loop(0, rows, step, tuple(state[h, :] for h in halves), unroll=8)
    for h, s in zip(halves, states):
        state[h, :] = s
    gate = branch(0)
    for i in range(tiles):
        cols = slice(i * lane, (i + 1) * lane)
        conv = modes[i, pl.ds(0, rows, stride=8), :]
        for s in range(1, 8):
            conv = conv + modes[i, pl.ds(s, rows, stride=8), :]
        out[0, :, cols] = (gate[:, cols] * conv).astype(out.dtype)


def run_conv(order, pick, parts, rows, taps, decay, scaled, state, halo):
    blocks = order.shape[0]
    width3 = taps.shape[1]
    width = width3 // 3
    mode_count = decay.shape[0]
    lane = min(128, width)

    def whole(shape):
        return pl.BlockSpec(shape, lambda i, order, pick: (0,) * len(shape))

    return pl.pallas_call(
        conv_kernel,
        out_shape=(
            jax.ShapeDtypeStruct((blocks, rows, width), jnp.bfloat16),
            jax.ShapeDtypeStruct((mode_count, width), jnp.float32),
            jax.ShapeDtypeStruct((8, width3), jnp.float32),
        ),
        grid_spec=pltpu.PrefetchScalarGridSpec(
            num_scalar_prefetch=2,
            grid=(blocks,),
            in_specs=[pl.BlockSpec((1, rows, width3), lambda i, order, pick: (order[i], 0, 0))] * len(parts)
            + [
                whole((3, width3)),
                whole((mode_count, width)),
                whole((mode_count, width)),
                whole((mode_count, width)),
                whole((8, width3)),
            ],
            out_specs=[
                pl.BlockSpec((1, rows, width), lambda i, order, pick: (i, 0, 0)),
                whole((mode_count, width)),
                whole((8, width3)),
            ],
            scratch_shapes=[
                pltpu.VMEM((rows + 8, width3), jnp.float32),
                pltpu.VMEM((rows, width), jnp.float32),
                pltpu.VMEM((width // lane, rows * 8, lane), jnp.float32),
            ],
        ),
        compiler_params=pltpu.CompilerParams(vmem_limit_bytes=16 * 1024 * 1024),
        cost_estimate=pl.CostEstimate(flops=0, bytes_accessed=0, transcendentals=0),
        name="conv",
    )(order, pick, *(p.reshape(-1, rows, width3) for p in parts), taps, decay, scaled, state, halo)


def cut_tokens_kernel(index, *refs):
    for i, source in enumerate(refs[:-1]):
        refs[-1][i] = source[...]


def cut_tokens(tokens, row_block, planes, rows):
    depth = tokens.shape[1] // planes

    def cut(i):
        return pl.BlockSpec((rows, depth), lambda n, index: (index[0], i))

    return pl.pallas_call(
        cut_tokens_kernel,
        out_shape=jax.ShapeDtypeStruct((planes, rows, depth), tokens.dtype),
        grid_spec=pltpu.PrefetchScalarGridSpec(
            num_scalar_prefetch=1,
            grid=(1,),
            in_specs=[cut(i) for i in range(planes)],
            out_specs=pl.BlockSpec((planes, rows, depth), lambda n, index: (0, 0, 0)),
        ),
        compiler_params=pltpu.CompilerParams(vmem_limit_bytes=48 * 1024 * 1024),
        cost_estimate=pl.CostEstimate(flops=0, bytes_accessed=0, transcendentals=0),
        name="cut_tokens",
    )(jnp.reshape(row_block, (1,)).astype(jnp.int32), *([tokens] * planes))


def cut_weight_kernel(index, *refs):
    width = refs[0].shape[2]
    for i, source in enumerate(refs[:-1]):
        refs[-1][:, i * width : (i + 1) * width] = source[0]


def cut_weight(weight, column_block, width, first_branch=0, branches=3):
    rows = weight.shape[1]
    if width % 128:
        cut = lax.dynamic_slice(weight, (first_branch, 0, column_block * width), (branches, rows, width))
        return jnp.transpose(cut, (1, 0, 2)).reshape(rows, branches * width)

    def cut(i):
        return pl.BlockSpec((1, rows, width), lambda n, index: (first_branch + i, 0, index[0]))

    return pl.pallas_call(
        cut_weight_kernel,
        out_shape=jax.ShapeDtypeStruct((rows, branches * width), weight.dtype),
        grid_spec=pltpu.PrefetchScalarGridSpec(
            num_scalar_prefetch=1,
            grid=(1,),
            in_specs=[cut(i) for i in range(branches)],
            out_specs=pl.BlockSpec((rows, branches * width), lambda n, index: (0, 0)),
        ),
        compiler_params=pltpu.CompilerParams(vmem_limit_bytes=48 * 1024 * 1024),
        cost_estimate=pl.CostEstimate(flops=0, bytes_accessed=0, transcendentals=0),
        name="cut_weight",
    )(jnp.reshape(column_block, (1,)).astype(jnp.int32), *([weight] * branches))


def chain_kernel(slots, planes, has_got, place, *refs):
    terms, refs = refs[: len(slots)], refs[len(slots) :]
    got, refs = (refs[0], refs[1:]) if has_got else (None, refs)
    held, sem = refs[-2:]
    total = refs[-3] if slots[-1] == planes - 1 else None
    sent = refs[-4 if total is not None else -3] if slots[0] < planes - 1 else None
    for slot, term in zip(slots, terms):

        @pl.when(place[0] == slot)
        def _(slot=slot, term=term):
            copy = pltpu.make_async_copy(term, held, sem)
            copy.start()
            copy.wait()
            value = held[...]
            if has_got:
                value = value + got[...].astype(jnp.float32)
            if slot == planes - 1:
                total[...] = value
            else:
                sent[...] = value.astype(sent.dtype)


def run_chain(place, slots, planes, terms, got, total):
    rows, width3 = terms[0].shape
    outs, aliases = [], {}
    inputs = [place, *terms] + ([got] if got is not None else [])
    if slots[0] < planes - 1:
        outs.append(jax.ShapeDtypeStruct((rows, width3), jnp.bfloat16))
    if slots[-1] == planes - 1:
        if total is not None:
            aliases = {len(inputs): len(outs)}
            inputs.append(total)
        outs.append(jax.ShapeDtypeStruct((rows, width3), jnp.float32))
    vmem = pl.BlockSpec(memory_space=pltpu.VMEM)
    specs = [pl.BlockSpec(memory_space=pltpu.SMEM)] + [pl.BlockSpec(memory_space=pl.ANY)] * len(terms)
    result = pl.pallas_call(
        functools.partial(chain_kernel, tuple(slots), planes, got is not None),
        out_shape=outs,
        in_specs=specs + [vmem] * (len(inputs) - len(specs)),
        out_specs=[vmem] * len(outs),
        scratch_shapes=[pltpu.VMEM((rows, width3), jnp.float32), pltpu.SemaphoreType.DMA],
        input_output_aliases=aliases,
        compiler_params=pltpu.CompilerParams(vmem_limit_bytes=8 * 1024 * 1024),
        cost_estimate=pl.CostEstimate(flops=0, bytes_accessed=0, transcendentals=0),
        name="chain",
    )(*inputs)
    sent = result[0] if slots[0] < planes - 1 else None
    return sent, (result[-1] if slots[-1] == planes - 1 else None)


def term_kernel(*refs):
    blocks, weight, out = refs[:-2], refs[-2], refs[-1]
    row = 0
    for block in blocks:
        rows = block.shape[0]
        out[row : row + rows, :] = jnp.dot(block[...], weight[...], preferred_element_type=jnp.float32)
        row += rows


def term(blocks, weight):
    depth, width = weight.shape
    rows = sum(b.shape[0] for b in blocks)
    step = width // 3 if width // 3 % 128 == 0 else width
    return pl.pallas_call(
        term_kernel,
        out_shape=jax.ShapeDtypeStruct((rows, width), jnp.float32),
        grid=(width // step,),
        in_specs=[pl.BlockSpec(b.shape, lambda n: (0, 0)) for b in blocks]
        + [pl.BlockSpec((depth, step), lambda n: (0, n))],
        out_specs=pl.BlockSpec((rows, step), lambda n: (0, n)),
        compiler_params=pltpu.CompilerParams(vmem_limit_bytes=16 * 1024 * 1024),
        cost_estimate=pl.CostEstimate(flops=0, bytes_accessed=0, transcendentals=0),
        name="term",
    )(*blocks, weight)


def join_kernel(first, second, out):
    half = first.shape[2]
    out[:, :half] = first[0]
    out[:, half:] = second[0]


def join(first, second, order):
    blocks, rows, half = first.shape
    if half % 128:
        both = jnp.stack([first, second]).reshape((2,) + order + (rows, half))
        return both.transpose(4, 2, 3, 1, 0, 5).reshape(rows, -1)
    xs, ys, cs = order

    def source(i):
        return (i % xs) * ys * cs + i // xs

    return pl.pallas_call(
        join_kernel,
        out_shape=jax.ShapeDtypeStruct((rows, 2 * blocks * half), first.dtype),
        grid=(blocks,),
        in_specs=[pl.BlockSpec((1, rows, half), lambda i: (source(i), 0, 0))] * 2,
        out_specs=pl.BlockSpec((rows, 2 * half), lambda i: (0, i)),
        compiler_params=pltpu.CompilerParams(vmem_limit_bytes=8 * 1024 * 1024),
        name="join",
    )(first, second)


def after(value, *others):
    return lax.optimization_barrier((value, *others))[0]


def ring(axis, k):
    count = lax.axis_size(axis)
    return [(s, (s + k) % count) for s in range(count)]


def gather_rel(value, axis):
    count = lax.axis_size(axis)
    pieces = [value] + [lax.ppermute(value, axis, ring(axis, k)) for k in range(1, count)]
    return jnp.concatenate(pieces, axis=0) if count > 1 else value


def shards(tokens, in_weight, short_taps, decay_rates, residues):
    Z, X, Y, C = (lax.axis_size(a) for a in ("z", "x", "y", "c"))
    z, x, y, c = (lax.axis_index(a) for a in ("z", "x", "y", "c"))
    tok_rows, depth = tokens.shape
    w_rows, _, chans = in_weight.shape
    own = chans // X
    half = own // 2
    plane_depth = X * w_rows

    lower = z < Z // 2
    far_block = jnp.where(lower, 0, 1)
    near_block = 1 - far_block

    weight = jnp.transpose(in_weight, (1, 0, 2))

    def sends(block, *branches):
        return [cut_weight(weight, 2 * ((x + k) % X) + block, half, *branches) for k in range(1, X)]

    def moved(pieces):
        return [lax.ppermute(p, "x", ring("x", k + 1)) for k, p in enumerate(pieces)]

    def assemble(kept, pieces):
        held = [kept] + pieces
        rows = []
        for i in range(X):
            row = held[0]
            for k in range(1, X):
                row = jnp.where((x - i) % X == k, held[k], row)
            rows.append(row)
        return jnp.concatenate(rows, axis=0)

    share = tok_rows // (Y * C)
    mine = cut_tokens(tokens, y * C + c, Z, share)
    far_sends = sends(far_block)
    far_got = moved([after(p, mine) for p in far_sends])
    split = lax.all_to_all(mine, "z", split_axis=0, concat_axis=0, tiled=True)
    near_sends = [sends(near_block, 0, 1), sends(near_block, 1, 2)]
    near_got = [moved([after(p, *far_got) for p in near_sends[0]]), None]
    kept = [cut_weight(weight, 2 * x + block, half) for block in (far_block, near_block)]
    def places(*sizes):
        grids = jnp.meshgrid(*(jnp.arange(n, dtype=jnp.int32) for n in sizes), indexing="ij")
        return [g.reshape(-1) for g in grids]

    bx, by, bc = places(X, Y, C)
    rel_x, rel_y, rel_c = (x - bx) % X, (y - by) % Y, (c - bc) % C
    group_rows = X * Y * C * share
    unit_rows = group_rows * Z // 8
    lead = [C * (X, Y)[k % 2] * share for k in range(Z)]

    def rows_of(k):
        column, inner = (rel_y, rel_x) if k % 2 == 0 else (rel_x, rel_y)
        head, tail = k * group_rows, k * group_rows + lead[k]
        if k < 2:
            head, tail = (0, lead[0] + lead[1]) if k == 0 else (lead[0], group_rows + lead[1])
        place = jnp.where(column == 0, head, tail + (column - 1) * lead[k])
        return place + rel_c * (lead[k] // C) + inner * share

    def near_cut(value):
        return lax.dynamic_slice_in_dim(value, x * own + near_block * half, half, axis=value.ndim - 1)

    taps = near_cut(short_taps).reshape(3, 3 * half)
    decay = near_cut(jnp.exp(-decay_rates))
    scaled = near_cut(residues * jnp.sqrt(2.0 * decay_rates))

    place_up = jnp.reshape(z, (1,)).astype(jnp.int32)
    place_down = Z - 1 - place_up
    orders = []
    for k in range(Z):
        first = 0 if k < 2 else k * group_rows // unit_rows
        rows = rows_of(k) - first * unit_rows
        orders.append((first, rows % unit_rows // share, rows // unit_rows))
    small = [taps, decay, scaled, place_up, place_down] + [v for o in orders for v in o[1:]]

    far_weight = assemble(kept[0], far_got)
    split = list(after(split, far_weight, *near_got[0], *near_sends[1], *kept, *small))
    near_weight = None

    pairs, others = [], []
    sent_ups = []

    def first_step(k, *before):
        pairs.append(gather_rel(after(split[k], *before), "xy"[k % 2]))

    def second_step(k, *before):
        axis = "yx"[k % 2]
        value = after(pairs[k], *before)
        others.append([lax.ppermute(value, axis, ring(axis, j)) for j in range(1, lax.axis_size(axis))])

    def add_planes(k):
        planes = range(k, min(k + 2, Z))
        for i in planes:
            first_step(i, *sent_ups[max(0, k - 2) : k - 1])
        if k == 0:
            pairs[:] = lax.optimization_barrier(tuple(pairs))
        for i in planes:
            second_step(i, *(sent_ups[k - 1 + i % 2 : k + i % 2] if k else []))

    count = group_rows * Z // unit_rows
    far, near = {}, {}
    ups, downs = {}, {}
    totals = []
    state = jnp.zeros_like(decay)
    halo = jnp.zeros((8, 3 * half), jnp.float32)
    outs = []
    before = []
    came, due = {}, {}

    blocks, columns, used = [], [], list(range(Z))
    add_planes(0)

    def unit(u):
        nonlocal blocks
        rows, have = [], 0
        while have < unit_rows:
            if not blocks:
                if not columns:
                    k = used.pop(0)
                    while len(pairs) <= k:
                        add_planes(len(pairs))
                    if k == 0:
                        columns.extend(pairs[:2] + others[0] + others[1])
                        used.pop(0)
                    else:
                        columns.extend([pairs[k]] + others[k])
                value = columns.pop(0)
                blocks = [value]
                if u > 0:
                    value = after(value, sent_ups[max(0, u - 2)])
                blocks += [lax.ppermute(value, "c", ring("c", j)) for j in range(1, C)]
            block = blocks.pop(0)
            if block.shape[0] > unit_rows - have:
                blocks.insert(0, block[unit_rows - have :])
                block = block[: unit_rows - have]
            rows.append(block)
            have += block.shape[0]
        rows[0] = after(rows[0], *sent_ups[u - 1 : u])
        return rows

    def ready(plane):
        return group_rows + lead[1] if plane == 0 else (plane + 1) * group_rows

    def emit(plane):
        nonlocal state, halo
        first, order, pick = orders[plane]
        parts = totals[first : -(-ready(plane) // unit_rows)]
        out, state, halo = run_conv(order, pick, parts, share, taps, decay, scaled, state, halo)
        outs.append(out.reshape(X * Y * C, share, half))
        return out

    for tick in range(count + 2 * (Z - 1)):
        slots = [s for s in range(Z) if 0 <= tick - 2 * s < count]
        if tick < count:
            value = unit(tick)
            far[tick] = term(value, far_weight)
            near[tick] = value
        u = tick - 2 * (Z // 2)
        if 0 <= u < count:
            if near_weight is None:
                near_got[1] = moved([after(p, *sent_ups[1:2]) for p in near_sends[1]])
                whole = [jnp.concatenate(p, axis=1) for p in zip(*near_got)]
                near_weight = assemble(kept[1], [after(p, *sent_ups[tick - 1 : tick]) for p in whole])
            value = after(near[u][0], *(sent_ups[tick - 1 : tick] or before))
            near[u] = term([value] + near[u][1:], near_weight)
        terms = [(far if s < Z // 2 else near)[tick - 2 * s] for s in slots]
        sent_up, total = run_chain(after(place_up, *before), slots, Z, terms, ups.get(tick - 2), None)
        if sent_up is not None:
            ups[tick] = lax.ppermute(sent_up, "z", [(s, s + 1) for s in slots if s + 1 < Z])
            sent_ups.append(sent_up)
        before = [total if sent_up is None else sent_up]
        sent_down, total = run_chain(after(place_down, *before), slots, Z, terms, downs.get(tick - 2), total)
        if sent_down is not None:
            downs[tick] = lax.ppermute(sent_down, "z", [(Z - 1 - s, Z - 2 - s) for s in slots if s + 1 < Z])
        before = [total if sent_down is None else sent_down] + due.pop(tick + 1, [])
        if total is not None:
            totals.append(total)
            if len(outs) < Z and len(totals) * unit_rows >= ready(len(outs)):
                k = len(outs)
                before.append(emit(k))
                for home in (0, Z - 1):
                    if 0 < abs(k - home) < Z - 1 and tick + 3 < count + 2 * (Z - 1):
                        came[home, k] = lax.ppermute(outs[k], "z", [(home, k)])
                        due.setdefault(count + 2 * (Z - 1) - 1, []).append(came[home, k])
    while len(outs) < Z:
        emit(len(outs))

    def collect(home):
        total = jnp.where(z == home, outs[home], jnp.zeros_like(outs[home]))
        for k in range(Z):
            if k != home:
                if (home, k) not in came:
                    value = after(outs[k], totals[-1]) if k == 0 else outs[k]
                    came[home, k] = lax.ppermute(value, "z", [(home, k)])
                total = total + came[home, k]
        return total

    def spread(total):
        return lax.all_to_all(total, ("x", "y", "c"), split_axis=0, concat_axis=0, tiled=True)

    upper = spread(collect(Z - 1))
    return join(upper, spread(after(collect(0), upper)), (X, Y, C))


def solution(mesh):
    ctx, ch = mesh.shape["ctx"], mesh.shape["ch"]
    xs = 1
    while 4 * xs * xs <= ctx:
        xs *= 2
    cs = 2 if ch % 2 == 0 else 1
    fine = Mesh(mesh.devices.reshape(ctx // xs, xs, ch // cs, cs), ("z", "x", "y", "c"))
    return jax.shard_map(
        shards,
        mesh=fine,
        in_specs=(
            P(("z", "x"), None),
            P(("z", "x"), None, ("y", "c")),
            P(None, None, ("y", "c")),
            P(None, ("y", "c")),
            P(None, ("y", "c")),
        ),
        out_specs=P(("z", "x", "y", "c"), None),
        check_vma=False,
    )
```
